512 devices in a mesh: sample: 8 (over y_hi, core), prefix: 64 (over x, y_lo, z).
Axes of the slice: x: 4, y: 8 (y_hi: 4, y_lo: 2; y = y_hi * 2 + y_lo), z: 8, core: 2. Of those that a mesh axis runs over, the one named last changes fastest.
Arguments:
- resp_q: bfloat16 [512, 128, 4096], P(('sample', 'prefix')), may hold values from -6 to 6
- resp_k: bfloat16 [512, 128, 512], P(('sample', 'prefix')), may hold values from -6 to 6
- resp_v: bfloat16 [512, 128, 512], P(('sample', 'prefix')), may hold values from -6 to 6
- resp_do: bfloat16 [512, 128, 4096], P(('sample', 'prefix')), may hold values from -6 to 6
- resp_out: bfloat16 [512, 128, 4096], P(('sample', 'prefix')), may hold values from -6 to 6
- resp_lse: float32 [512, 128, 32], P(('sample', 'prefix'))
- prompt_k: bfloat16 [1024, 512], P('prefix'), may hold values from -6 to 6
- prompt_v: bfloat16 [1024, 512], P('prefix'), may hold values from -6 to 6
- resp_lengths: int32 [512], P(('sample', 'prefix')), may hold values from 16 to 128, as said below
Outputs:
- resp_dq: bfloat16 [512, 128, 4096], P(('sample', 'prefix'))
- resp_dk: bfloat16 [512, 128, 512], P(('sample', 'prefix'))
- resp_dv: bfloat16 [512, 128, 512], P(('sample', 'prefix'))
- prompt_dk: float32 [1024, 512], P('prefix')
- prompt_dv: float32 [1024, 512], P('prefix')
The draws below stay inside these ranges and needn't reach their ends.
Inputs may be any that keep to these rules, and one draw needn't show every extreme that they name: `resp_lengths`: some response has exactly 128 live tokens and some has 16.
All inputs are finite; a program needn't handle non-finite values.
Results may differ from the reference program's by a relative error of at most 0.0051.
Values may be sent and summed in bfloat16 or wider, within the bound.
No kernel may reach another device: no remote copies, remote signals or barrier semaphores. Data moves between devices by JAX's collectives and lax.ppermute only.
A program may use at most 64 MiB of HBM per device.

```python
import jax
import jax.numpy as jnp
from jax import lax

H = 32
KVH = 4
HD = 128
R = 128
RESP = 512
P_SIZE = 1024


def draw_resp_lse(key, part):
    key = jax.random.fold_in(key, 11)
    positions = jnp.arange(R, dtype=jnp.float32)
    baseline = jnp.log(P_SIZE + positions + 1.0)[None, :, None]
    offset = 0.5 + jnp.clip(0.25 * jax.random.normal(key, (RESP, R, H), jnp.float32), -0.5, 0.5)
    return baseline + offset


def draw_resp_lengths(key, part):
    key = jax.random.fold_in(key, 23)
    first_key, second_key = jax.random.split(key)
    picked = jax.random.randint(first_key, (RESP,), R // 8, R + 1)
    order = jax.random.permutation(second_key, RESP)
    picked = picked.at[order[0]].set(R)
    picked = picked.at[order[1]].set(R // 8)
    return picked.astype(jnp.int32)


def steps_of(key, shape, pieces, low, top_value):
    level = 1.0
    for position, blocks in pieces:
        draws = jax.random.uniform(jax.random.fold_in(jax.random.fold_in(key, 6), position), (blocks,), jnp.float32, low / len(pieces), top_value / len(pieces))
        level = level * jnp.repeat(jnp.exp(draws), shape[position] // blocks).reshape((-1,) + (1,) * (len(shape) - 1 - position))
    return level


def scatter_about(stream_key, dims, deviation, bound, cuts=(), kind=jnp.bfloat16):
    gain = steps_of(stream_key, dims, cuts, -0.22, 0.18) if cuts else 1.0
    values = jax.random.normal(stream_key, dims, jnp.float32) * deviation * gain
    return jnp.minimum(jnp.maximum(values, -bound), bound).astype(kind)


def setup_inputs(seed: int = 0) -> dict:
    splits = jax.random.split(jax.random.key(seed), 10)
    resp_q = scatter_about(splits[0], (RESP, R, H * HD), 1.0, 6.0, ((0, 512),))
    resp_k = scatter_about(splits[1], (RESP, R, KVH * HD), 1.0, 6.0, ((0, 512),))
    resp_v = scatter_about(splits[2], (RESP, R, KVH * HD), 1.0, 6.0, ((0, 512),))
    resp_do = scatter_about(splits[3], (RESP, R, H * HD), 1.0, 6.0, ((0, 512),))
    resp_out = scatter_about(splits[4], (RESP, R, H * HD), 1.0, 6.0, ((0, 512),))
    resp_lse = draw_resp_lse(jax.random.fold_in(splits[9], 71), 0)
    prompt_k = scatter_about(splits[6], (P_SIZE, KVH * HD), 1.0, 6.0, ((0, 64),))
    prompt_v = scatter_about(splits[7], (P_SIZE, KVH * HD), 1.0, 6.0, ((0, 64),))
    resp_lengths = draw_resp_lengths(jax.random.fold_in(splits[9], 71), 0)
    return {"resp_q": resp_q, "resp_k": resp_k, "resp_v": resp_v, "resp_do": resp_do, "resp_out": resp_out, "resp_lse": resp_lse, "prompt_k": prompt_k, "prompt_v": prompt_v, "resp_lengths": resp_lengths}


def reference(resp_q, resp_k, resp_v, resp_do, resp_out, resp_lse, prompt_k, prompt_v, resp_lengths):
    groups = H // KVH
    score_scale = HD ** -0.5
    key_count = P_SIZE + R
    query_pos = jnp.arange(R, dtype=jnp.int32)
    key_pos = jnp.arange(key_count, dtype=jnp.int32)

    def one_response(response_items):
        queries, own_keys, own_values, grad_out, fwd_out, lse_rows, length = response_items
        all_keys = jnp.concatenate([prompt_k, own_keys], 0).astype(jnp.float32).reshape(key_count, KVH, HD).transpose(1, 0, 2)
        all_values = jnp.concatenate([prompt_v, own_values], 0).astype(jnp.float32).reshape(key_count, KVH, HD).transpose(1, 0, 2)
        live = (query_pos[:, None] < length) & ((key_pos[None, :] < P_SIZE) | (key_pos[None, :] - P_SIZE <= query_pos[:, None]))
        live_mask = live.astype(jnp.float32)
        query_heads = queries.astype(jnp.float32).reshape(R, KVH, groups, HD).transpose(1, 0, 2, 3)
        grad_heads = grad_out.astype(jnp.float32).reshape(R, KVH, groups, HD).transpose(1, 0, 2, 3)
        out_heads = fwd_out.astype(jnp.float32).reshape(R, KVH, groups, HD).transpose(1, 0, 2, 3)
        out_dot = jnp.sum(grad_heads * out_heads, -1)
        lse_heads = lse_rows.reshape(R, KVH, groups).transpose(1, 0, 2)

        def per_group(group_items):
            query_x, grad_x, key_x, value_x, dot_x, lse_x = group_items
            scores = jnp.einsum('tgd,ud->gtu', query_x, key_x) * score_scale
            probs = jnp.exp(scores - lse_x.T[:, :, None]) * live_mask[None]
            prob_grad = jnp.einsum('tgd,ud->gtu', grad_x, value_x)
            score_grad = probs * (prob_grad - dot_x.T[:, :, None])
            probs_low = lax.optimization_barrier(probs.astype(jnp.bfloat16)).astype(jnp.float32)
            score_low = lax.optimization_barrier(score_grad.astype(jnp.bfloat16)).astype(jnp.float32)
            query_grad = jnp.einsum('gtu,ud->tgd', score_low, key_x) * score_scale
            key_grad = jnp.einsum('gtu,tgd->ud', score_low, query_x) * score_scale
            value_grad = jnp.einsum('gtu,tgd->ud', probs_low, grad_x)
            return query_grad, key_grad, value_grad

        query_grad, key_grad, value_grad = lax.map(per_group, (query_heads, grad_heads, all_keys, all_values, out_dot, lse_heads))
        query_grad = query_grad.transpose(1, 0, 2, 3).reshape(R, H * HD).astype(jnp.bfloat16)
        key_grad = key_grad.transpose(1, 0, 2).reshape(key_count, KVH * HD)
        value_grad = value_grad.transpose(1, 0, 2).reshape(key_count, KVH * HD)
        return query_grad, key_grad[P_SIZE:].astype(jnp.bfloat16), value_grad[P_SIZE:].astype(jnp.bfloat16), key_grad[:P_SIZE], value_grad[:P_SIZE]

    def accumulate(carry, response_items):
        outputs = one_response(response_items)
        return (carry[0] + outputs[3], carry[1] + outputs[4]), (outputs[0], outputs[1], outputs[2])

    start = (jnp.zeros((P_SIZE, KVH * HD), jnp.float32), jnp.zeros((P_SIZE, KVH * HD), jnp.float32))
    sums, per_resp = lax.scan(accumulate, start, (resp_q, resp_k, resp_v, resp_do, resp_out, resp_lse, resp_lengths))
    return per_resp[0], per_resp[1], per_resp[2], sums[0], sums[1]
```

```python
import functools
import math

import jax
import jax.numpy as jnp
from jax import lax
from jax.experimental import pallas as pl
from jax.experimental.pallas import tpu as pltpu
from jax.sharding import Mesh
from jax.sharding import PartitionSpec as P

H = 32
KVH = 4
HD = 128
R = 128
G = H // KVH
QR = G * R
SCALE = HD**-0.5
LOG2E = math.log2(math.e)
AXES = ("yh", "core", "x", "yl", "zh", "zl")
f32 = jnp.float32
bf16 = jnp.bfloat16

OFF_DO = QR
OFF_K = 2 * QR
OFF_V = OFF_K + R
OFF_ST = OFF_V + R
PACK = OFF_ST + 6 * G

NT = (((1,), (1,)), ((), ()))
NN = (((1,), (0,)), ((), ()))
VMEM = pl.BlockSpec(memory_space=pltpu.VMEM)
CHUNK = 512


def dot(a, b, dims):
    return lax.dot_general(a, b, dims, preferred_element_type=f32)


def split3(value):
    hi = value.astype(bf16)
    rest = value - hi.astype(f32)
    mid = rest.astype(bf16)
    low = (rest - mid.astype(f32)).astype(bf16)
    return hi, mid, low


def prep_kernel(info, q, do, out, k, v, lse, send, mine):
    step = pl.program_id(0)
    length = info[1]

    def fill(ref):
        ones = jnp.ones((8, HD), bf16)
        rows = []
        for h in range(G):
            cols = slice(h * HD, (h + 1) * HD)
            rs = slice(h * R, (h + 1) * R)
            ref[0, rs, :] = q[:, cols]
            dh = do[:, cols]
            ref[0, OFF_DO + h * R : OFF_DO + (h + 1) * R, :] = dh
            prod = dh.astype(f32) * out[:, cols].astype(f32)
            hi = prod.astype(bf16)
            low = (prod - hi.astype(f32)).astype(bf16)
            rows.append((dot(ones, hi, NT) + dot(ones, low, NT))[0:1, :])
        ref[0, OFF_K : OFF_K + R, :] = k[...]
        ref[0, OFF_V : OFF_V + R, :] = v[...]
        delta = jnp.concatenate(rows, 0)
        token = lax.broadcasted_iota(jnp.int32, (G, R), 1)
        lse2 = jnp.where(token < length, lse[...] * LOG2E, 1e30)
        ref[0, OFF_ST:PACK, :] = jnp.concatenate(split3(lse2) + split3(delta), 0)

    @pl.when(step < 2)
    def _():
        fill(send)

    @pl.when(step >= 2)
    def _():
        fill(mine)


def prep(core, length, q, do, out, k, v, lse_t):
    def head(i, info):
        return jnp.where(i < 2, 2 * (1 - info[0]) + i, 2 * info[0] + i - 2)

    wide = pl.BlockSpec((R, QR), lambda i, info: (0, head(i, info)))
    narrow = pl.BlockSpec((R, HD), lambda i, info: (0, head(i, info)))
    shape = jax.ShapeDtypeStruct((2, PACK, HD), bf16)
    return pl.pallas_call(
        prep_kernel,
        out_shape=(shape, shape),
        grid_spec=pltpu.PrefetchScalarGridSpec(
            num_scalar_prefetch=1,
            grid=(4,),
            in_specs=[wide, wide, wide, narrow, narrow, pl.BlockSpec((G, R), lambda i, info: (head(i, info), 0))],
            out_specs=(
                pl.BlockSpec((1, PACK, HD), lambda i, info: (jnp.minimum(i, 1), 0, 0)),
                pl.BlockSpec((1, PACK, HD), lambda i, info: (jnp.maximum(i - 2, 0), 0, 0)),
            ),
        ),
        compiler_params=pltpu.CompilerParams(vmem_limit_bytes=20 * 2**20),
        cost_estimate=pl.CostEstimate(flops=10**7, bytes_accessed=6 * 2**20, transcendentals=0),
        name="prep",
    )(jnp.stack([core, length]), q, do, out, k, v, lse_t)


def stat_row(ref, g, kind, first, count):
    base = OFF_ST + kind * 3 * G
    block = [ref[g, base + term * G : base + (term + 1) * G, :].astype(f32) for term in range(3)]
    total = block[0] + block[1] + block[2]
    return jnp.concatenate([total[h : h + 1, :] for h in range(first, first + count)], 1)


def tile_grads(ref, g, chunk, keys, values, causal):
    cs = slice(chunk * CHUNK, (chunk + 1) * CHUNK)
    qc = ref[g, cs, :]
    dc = ref[g, OFF_DO + chunk * CHUNK : OFF_DO + (chunk + 1) * CHUNK, :]
    heads = CHUNK // R
    lse2 = stat_row(ref, g, 0, chunk * heads, heads)
    delta = stat_row(ref, g, 1, chunk * heads, heads)
    scores = dot(keys, qc, NT)
    prob_grad = dot(values, dc, NT)
    probs = jnp.exp2(scores * (SCALE * LOG2E) - lse2)
    if causal:
        shape = scores.shape
        token = lax.broadcasted_iota(jnp.int32, shape, 1) % R
        probs = jnp.where(lax.broadcasted_iota(jnp.int32, shape, 0) <= token, probs, 0.0)
    score_low = (probs * (prob_grad - delta)).astype(bf16)
    dv = dot(probs.astype(bf16), dc, NN)
    dk = dot(score_low, qc, NN)
    dq = lax.dot_general(keys, score_low, (((0,), (0,)), ((), ())), preferred_element_type=f32).T
    return dk, dv, dq, cs


def own_kernel(mine, recv, dq, grads):
    for r, ref in enumerate((mine, recv)):
        for g in range(2):
            keys = ref[g, OFF_K : OFF_K + R, :]
            values = ref[g, OFF_V : OFF_V + R, :]
            dk = jnp.zeros((R, HD), f32)
            dv = jnp.zeros((R, HD), f32)
            for chunk in range(QR // CHUNK):
                dk_c, dv_c, dq_c, cs = tile_grads(ref, g, chunk, keys, values, True)
                dk += dk_c
                dv += dv_c
                dq[r, g, cs, :] = dq_c
            grads[r, :, g * HD : (g + 1) * HD] = (dk * SCALE).astype(bf16)
            grads[r, :, (2 + g) * HD : (3 + g) * HD] = dv.astype(bf16)


def prompt_block(mine, recv, kv, emit_dq, out):
    for g in range(2):
        keys = kv[:, g * HD : (g + 1) * HD]
        values = kv[:, (2 + g) * HD : (3 + g) * HD]
        rows = kv.shape[0]
        dk = jnp.zeros((rows, HD), f32)
        dv = jnp.zeros((rows, HD), f32)
        for r, ref in enumerate((mine, recv)):
            for chunk in range(QR // CHUNK):
                dk_c, dv_c, dq_c, cs = tile_grads(ref, g, chunk, keys, values, False)
                dk += dk_c
                dv += dv_c
                emit_dq(r, g, chunk, cs, dq_c)
        out[:, g * HD : (g + 1) * HD] = (dk * SCALE).astype(out.dtype)
        out[:, (2 + g) * HD : (3 + g) * HD] = dv.astype(out.dtype)


def block_kernel(mine, recv, kv, dq_in, dq, out):
    def emit_dq(r, g, chunk, cs, value):
        dq[r, g, cs, :] = dq_in[r, g, cs, :] + value

    prompt_block(mine, recv, kv, emit_dq, out)


def last_kernel(mine, recv, kv, dq_in, grads, own, back, out):
    def emit_dq(r, g, chunk, cs, value):
        total = ((dq_in[r, g, cs, :] + value) * SCALE).astype(bf16)
        target = own if r == 0 else back
        for j in range(CHUNK // R):
            h = g * G + chunk * (CHUNK // R) + j
            target[:, h * HD : (h + 1) * HD] = total[j * R : (j + 1) * R, :]

    prompt_block(mine, recv, kv, emit_dq, out)
    back[:, 2 * QR :] = grads[1]


def cost(rows):
    return pl.CostEstimate(
        flops=5 * 2 * rows * 4 * QR * HD, bytes_accessed=8 * 2**20, transcendentals=rows * 4 * QR
    )


PARAMS = pltpu.CompilerParams(vmem_limit_bytes=24 * 2**20)


def body(resp_q, resp_k, resp_v, resp_do, resp_out, resp_lse, prompt_k, prompt_v, resp_lengths):
    core = lax.axis_index("core").astype(jnp.int32)
    rows = prompt_k.shape[0]
    half = 2 * HD

    send, mine = prep(
        core, resp_lengths[0], resp_q[0], resp_do[0], resp_out[0], resp_k[0], resp_v[0], resp_lse[0].T
    )
    recv = lax.ppermute(send, "core", [(0, 1), (1, 0)])

    shard = jnp.concatenate(
        [
            lax.dynamic_slice_in_dim(prompt_k, core * half, half, 1),
            lax.dynamic_slice_in_dim(prompt_v, core * half, half, 1),
        ],
        1,
    )
    inner = ("yl", "zh", "zl")
    kv0 = lax.all_to_all(jnp.tile(shard, (16, 1)), inner, 0, 0, tiled=True)

    def along_x(value, shift):
        return lax.ppermute(value, "x", [(i, (i + shift) % 4) for i in range(4)])

    block_rows = 16 * rows
    blocks = {shift: along_x(kv0, -shift) for shift in (1, 3, 2)}
    dq_shape = jax.ShapeDtypeStruct((2, 2, QR, HD), f32)
    part_shape = jax.ShapeDtypeStruct((block_rows, 4 * HD), bf16)
    dq, grads = pl.pallas_call(
        own_kernel,
        out_shape=(dq_shape, jax.ShapeDtypeStruct((2, R, 4 * HD), bf16)),
        in_specs=[VMEM] * 2,
        out_specs=(VMEM,) * 2,
        compiler_params=PARAMS,
        cost_estimate=cost(R),
        name="own_keys",
    )(mine, recv)
    parts = []
    for shift in (1, 3, 2):
        dq, part = pl.pallas_call(
            block_kernel,
            out_shape=(dq_shape, part_shape),
            in_specs=[VMEM] * 4,
            out_specs=(VMEM,) * 2,
            input_output_aliases={3: 0},
            compiler_params=PARAMS,
            cost_estimate=cost(block_rows),
            name="prompt_block",
        )(mine, recv, blocks[shift], dq)
        parts.append(along_x(part, shift))
    own_dq, back, part0 = pl.pallas_call(
        last_kernel,
        out_shape=(
            jax.ShapeDtypeStruct((R, 2 * QR), bf16),
            jax.ShapeDtypeStruct((R, 2 * QR + 4 * HD), bf16),
            jax.ShapeDtypeStruct((block_rows, 4 * HD), f32),
        ),
        in_specs=[VMEM] * 5,
        out_specs=(VMEM,) * 3,
        compiler_params=PARAMS,
        cost_estimate=cost(block_rows),
        name="prompt_last",
    )(mine, recv, kv0, dq, grads)
    got = lax.ppermute(back, "core", [(0, 1), (1, 0)])

    total = (part0 + (parts[0].astype(f32) + parts[1].astype(f32)) + parts[2].astype(f32)).astype(bf16)
    total = lax.all_to_all(total, inner, 0, 0, tiled=True)
    total = jnp.sum(total.reshape(16, rows, 4 * HD).astype(f32), 0).astype(bf16)
    total = lax.all_to_all(jnp.tile(total, (8, 1)), ("yh", "core"), 0, 0, tiled=True)
    total = jnp.sum(total.reshape(4, 2, rows, 2, 2, HD).astype(f32), 0)
    prompt_dk = total[:, :, 0].transpose(1, 0, 2, 3).reshape(rows, KVH * HD)
    prompt_dv = total[:, :, 1].transpose(1, 0, 2, 3).reshape(rows, KVH * HD)

    def join(first, second):
        return jnp.where(
            core == 0, jnp.concatenate([first, second], -1), jnp.concatenate([second, first], -1)
        )[None]

    resp_dq = join(own_dq, got[:, : 2 * QR])
    resp_dk = join(grads[0][:, :half], got[:, 2 * QR : 2 * QR + half])
    resp_dv = join(grads[0][:, half:], got[:, 2 * QR + half :])
    return resp_dq, resp_dk, resp_dv, prompt_dk, prompt_dv


def solution(mesh):
    fine = Mesh(mesh.devices.reshape(4, 2, 4, 2, 4, 2), AXES)
    both = P(AXES, None, None)
    prefix = P(("x", "yl", "zh", "zl"), None)
    return jax.shard_map(
        body,
        mesh=fine,
        in_specs=(both,) * 6 + (prefix, prefix, P(AXES)),
        out_specs=(both, both, both, prefix, prefix),
        check_vma=False,
    )
```

```python
import functools
import math

import jax
import jax.numpy as jnp
from jax import lax
from jax.experimental import pallas as pl
from jax.experimental.pallas import tpu as pltpu
from jax.sharding import Mesh
from jax.sharding import PartitionSpec as P

H = 32
KVH = 4
HD = 128
R = 128
G = H // KVH
QR = G * R
SCALE = HD**-0.5
LOG2E = math.log2(math.e)
AXES = ("yh", "core", "x", "yl", "zh", "zl")
f32 = jnp.float32
bf16 = jnp.bfloat16

OFF_DO = QR
OFF_K = 2 * QR
OFF_V = OFF_K + R
OFF_ST = OFF_V + R
PACK = OFF_ST + 6 * G

NT = (((1,), (1,)), ((), ()))
NN = (((1,), (0,)), ((), ()))
VMEM = pl.BlockSpec(memory_space=pltpu.VMEM)
SMEM = pl.BlockSpec(memory_space=pltpu.SMEM)
ANY = pl.BlockSpec(memory_space=pl.ANY)
FLIPS = (2, 1, 3)
CHUNK = 512


def dot(a, b, dims):
    return lax.dot_general(a, b, dims, preferred_element_type=f32)


def split3(value):
    hi = value.astype(bf16)
    rest = value - hi.astype(f32)
    mid = rest.astype(bf16)
    low = (rest - mid.astype(f32)).astype(bf16)
    return hi, mid, low


def prep_kernel(info, q, do, out, k, v, lse, order_by, send, mine, q_buf, do_buf, out_buf, k_buf, v_buf, sems, kv_sems):
    core = info[0]
    length = info[1]
    order = (2 * (1 - core), 2 * (1 - core) + 1, 2 * core, 2 * core + 1)
    wide = [
        [
            pltpu.make_async_copy(src.at[:, pl.ds(pl.multiple_of(g * QR, QR), QR)], buf.at[i], sems.at[j, i])
            for j, (src, buf) in enumerate(((q, q_buf), (do, do_buf), (out, out_buf)))
        ]
        for i, g in enumerate(order)
    ]
    narrow = [pltpu.make_async_copy(k, k_buf, kv_sems.at[0]), pltpu.make_async_copy(v, v_buf, kv_sems.at[1])]
    for copies in [narrow] + wide:
        for copy in copies:
            copy.start()
    for copy in narrow:
        copy.wait()
    ones = jnp.ones((8, HD), bf16)
    token = lax.broadcasted_iota(jnp.int32, (G, R), 1)
    for i, g in enumerate(order):
        ref = send if i < 2 else mine
        s = i % 2
        for copy in wide[i]:
            copy.wait()
        rows = []
        for h in range(G):
            cols = slice(h * HD, (h + 1) * HD)
            ref[s, h * R : (h + 1) * R, :] = q_buf[i, :, cols]
            dh = do_buf[i, :, cols]
            ref[s, OFF_DO + h * R : OFF_DO + (h + 1) * R, :] = dh
            prod = dh.astype(f32) * out_buf[i, :, cols].astype(f32)
            hi = prod.astype(bf16)
            low = (prod - hi.astype(f32)).astype(bf16)
            rows.append((dot(ones, hi, NT) + dot(ones, low, NT))[0:1, :])
        head = pl.ds(pl.multiple_of(g * HD, HD), HD)
        ref[s, OFF_K : OFF_K + R, :] = k_buf[:, head]
        ref[s, OFF_V : OFF_V + R, :] = v_buf[:, head]
        delta = jnp.concatenate(rows, 0)
        lse_g = lse[pl.ds(pl.multiple_of(g * G, G), G), :]
        lse2 = jnp.where(token < length, lse_g * LOG2E, 1e30)
        ref[s, OFF_ST:PACK, :] = jnp.concatenate(split3(lse2) + split3(delta), 0)


def prep(core, length, q, do, out, k, v, lse_t, order_by):
    shape = jax.ShapeDtypeStruct((2, PACK, HD), bf16)
    whole = pl.BlockSpec(memory_space=pl.ANY)
    wide = pltpu.VMEM((4, R, QR), bf16)
    narrow = pltpu.VMEM((R, KVH * HD), bf16)
    return pl.pallas_call(
        prep_kernel,
        out_shape=(shape, shape),
        in_specs=[pl.BlockSpec(memory_space=pltpu.SMEM)] + [whole] * 5 + [VMEM, whole],
        out_specs=(VMEM, VMEM),
        scratch_shapes=[wide, wide, wide, narrow, narrow, pltpu.SemaphoreType.DMA((3, 4)), pltpu.SemaphoreType.DMA((2,))],
        compiler_params=pltpu.CompilerParams(vmem_limit_bytes=61 * 2**20),
        cost_estimate=pl.CostEstimate(flops=10**7, bytes_accessed=8 * 2**20, transcendentals=0),
        name="prep",
    )(jnp.stack([core, length]), q, do, out, k, v, lse_t, order_by)


def stat_row(ref, g, kind, first, count):
    base = OFF_ST + kind * 3 * G
    block = [ref[g, base + term * G : base + (term + 1) * G, :].astype(f32) for term in range(3)]
    total = block[0] + block[1] + block[2]
    return jnp.concatenate([total[h : h + 1, :] for h in range(first, first + count)], 1)


def tile_grads(ref, g, chunk, keys, values, causal):
    cs = slice(chunk * CHUNK, (chunk + 1) * CHUNK)
    qc = ref[g, cs, :]
    dc = ref[g, OFF_DO + chunk * CHUNK : OFF_DO + (chunk + 1) * CHUNK, :]
    heads = CHUNK // R
    lse2 = stat_row(ref, g, 0, chunk * heads, heads)
    delta = stat_row(ref, g, 1, chunk * heads, heads)
    scores = dot(keys, qc, NT)
    prob_grad = dot(values, dc, NT)
    probs = jnp.exp2(scores * (SCALE * LOG2E) - lse2)
    if causal:
        shape = scores.shape
        token = lax.broadcasted_iota(jnp.int32, shape, 1) % R
        probs = jnp.where(lax.broadcasted_iota(jnp.int32, shape, 0) <= token, probs, 0.0)
    score_low = (probs * (prob_grad - delta)).astype(bf16)
    dv = dot(probs.astype(bf16), dc, NN)
    dk = dot(score_low, qc, NN)
    dq = lax.dot_general(keys, score_low, (((0,), (0,)), ((), ())), preferred_element_type=f32).T
    return dk, dv, dq, cs


def prompt_block(mine, recv, kv, emit_dq, out):
    rows = kv.shape[0]
    for g in range(2):
        keys = kv[:, g * HD : (g + 1) * HD]
        values = kv[:, (2 + g) * HD : (3 + g) * HD]
        dk = jnp.zeros((rows, HD), f32)
        dv = jnp.zeros((rows, HD), f32)
        for r, ref in enumerate((mine, recv)):
            for chunk in range(QR // CHUNK):
                dk_c, dv_c, dq_c, cs = tile_grads(ref, g, chunk, keys, values, False)
                dk += dk_c
                dv += dv_c
                emit_dq(r, g, cs, dq_c)
        out[:, g * HD : (g + 1) * HD] = (dk * SCALE).astype(out.dtype)
        out[:, (2 + g) * HD : (3 + g) * HD] = dv.astype(out.dtype)


def first_kernel(mine, recv, kv, dq, grads, out):
    for r, ref in enumerate((mine, recv)):
        for g in range(2):
            keys = ref[g, OFF_K : OFF_K + R, :]
            values = ref[g, OFF_V : OFF_V + R, :]
            dk = jnp.zeros((R, HD), f32)
            dv = jnp.zeros((R, HD), f32)
            for chunk in range(QR // CHUNK):
                dk_c, dv_c, dq_c, cs = tile_grads(ref, g, chunk, keys, values, True)
                dk += dk_c
                dv += dv_c
                dq[r, g, cs, :] = dq_c
            grads[r, :, g * HD : (g + 1) * HD] = (dk * SCALE).astype(bf16)
            grads[r, :, (2 + g) * HD : (3 + g) * HD] = dv.astype(bf16)

    def emit_dq(r, g, cs, value):
        dq[r, g, cs, :] += value

    prompt_block(mine, recv, kv, emit_dq, out)


def middle_kernel(mine, recv, kv_a, kv_b, dq_in, dq, out_a, out_b):
    def emit_a(r, g, cs, value):
        dq[r, g, cs, :] = dq_in[r, g, cs, :] + value

    def emit_b(r, g, cs, value):
        dq[r, g, cs, :] += value

    prompt_block(mine, recv, kv_a, emit_a, out_a)
    prompt_block(mine, recv, kv_b, emit_b, out_b)


def last_kernel(core, mine, recv, kv, dq_in, grads, order_by, back, out, full_dq, full_dk, full_dv, own, sems):
    def emit_dq(r, g, cs, value):
        total = ((dq_in[r, g, cs, :] + value) * SCALE).astype(bf16)
        target = own if r == 0 else back
        for j in range(CHUNK // R):
            h = g * G + cs.start // R + j
            target[:, h * HD : (h + 1) * HD] = total[j * R : (j + 1) * R, :]

    def place(full, width):
        return full.at[:, pl.ds(pl.multiple_of(core[0] * width, width), width)]

    half = 2 * HD
    copies = [
        pltpu.make_async_copy(grads.at[0, :, :half], place(full_dk, half), sems.at[0]),
        pltpu.make_async_copy(grads.at[0, :, half:], place(full_dv, half), sems.at[1]),
        pltpu.make_async_copy(own, place(full_dq, 2 * QR), sems.at[2]),
    ]
    copies[0].start()
    copies[1].start()
    prompt_block(mine, recv, kv, emit_dq, out)
    copies[2].start()
    back[:, 2 * QR :] = grads[1]
    for copy in copies:
        copy.wait()


def join_kernel(core, got, in_dq, in_dk, in_dv, full_dq, full_dk, full_dv, sems):
    half = 2 * HD
    other = 1 - core[0]
    copies = []
    for i, (full, start, width) in enumerate(
        ((full_dq, 0, 2 * QR), (full_dk, 2 * QR, half), (full_dv, 2 * QR + half, half))
    ):
        place = full.at[:, pl.ds(pl.multiple_of(other * width, width), width)]
        copies.append(pltpu.make_async_copy(got.at[:, start : start + width], place, sems.at[i]))
    for copy in copies:
        copy.start()
    for copy in copies:
        copy.wait()


def same_kernel(x, y, o, p):
    pass


def shard_kernel(core, k, v, o):
    rows = k.shape[0]
    cols = pl.ds(pl.multiple_of(core[0] * 2 * HD, 2 * HD), 2 * HD)
    shard = jnp.concatenate([k[:, cols], v[:, cols]], 1)
    for i in range(o.shape[0] // rows):
        o[i * rows : (i + 1) * rows, :] = shard


def sum_blocks_kernel(a, b, c, d, back_in, o, back):
    o[...] = (a[...] + b[...].astype(f32) + c[...].astype(f32) + d[...].astype(f32)).astype(bf16)


def sum_copies_kernel(x, o):
    rows = 16
    total = x[0:rows, :].astype(f32)
    for i in range(1, x.shape[0] // rows):
        total += x[i * rows : (i + 1) * rows, :].astype(f32)
    total = total.astype(bf16)
    for i in range(o.shape[0] // rows):
        o[i * rows : (i + 1) * rows, :] = total


def sum_samples_kernel(x, dk, dv):
    rows = 16
    half = 2 * HD
    for c in range(2):
        total = x[c * rows : (c + 1) * rows, :].astype(f32)
        for y in range(1, 4):
            at = (2 * y + c) * rows
            total += x[at : at + rows, :].astype(f32)
        dk[:, c * half : (c + 1) * half] = total[:, :half]
        dv[:, c * half : (c + 1) * half] = total[:, half:]


def simple(kernel, out_shape, name, *args, in_specs=None, out_specs=None, limit=16, **options):
    single = not isinstance(out_shape, tuple)
    return pl.pallas_call(
        kernel,
        out_shape=out_shape,
        in_specs=in_specs or [VMEM] * len(args),
        out_specs=out_specs or (VMEM if single else (VMEM,) * len(out_shape)),
        compiler_params=pltpu.CompilerParams(vmem_limit_bytes=limit * 2**20),
        name=name,
        **options,
    )(*args)


def cost(rows):
    return pl.CostEstimate(
        flops=5 * 2 * rows * 4 * QR * HD, bytes_accessed=8 * 2**20, transcendentals=rows * 4 * QR
    )


PARAMS = pltpu.CompilerParams(vmem_limit_bytes=24 * 2**20)


def body(resp_q, resp_k, resp_v, resp_do, resp_out, resp_lse, prompt_k, prompt_v, resp_lengths):
    core = lax.axis_index("core").astype(jnp.int32)
    rows = prompt_k.shape[0]
    outer = ("yl", "zh", "zl")
    inner = "x"

    shards = simple(
        shard_kernel,
        jax.ShapeDtypeStruct((16 * rows, 4 * HD), bf16),
        "shards",
        core[None],
        prompt_k,
        prompt_v,
        in_specs=[SMEM, VMEM, VMEM],
        limit=61,
    )
    kv0 = lax.all_to_all(shards, outer, 0, 0, tiled=True)
    send, mine = prep(
        core,
        resp_lengths[0],
        resp_q[0],
        resp_do[0],
        resp_out[0],
        resp_k[0],
        resp_v[0],
        resp_lse[0].T,
        shards,
    )
    kv0, send = simple(
        same_kernel,
        (jax.ShapeDtypeStruct(kv0.shape, bf16), jax.ShapeDtypeStruct(send.shape, bf16)),
        "gathered_and_prepared",
        kv0,
        send,
        in_specs=[ANY, ANY],
        out_specs=(ANY, ANY),
        input_output_aliases={0: 0, 1: 1},
        limit=63,
    )
    recv = lax.ppermute(send, "core", [(0, 1), (1, 0)])

    def along(value, flip):
        return lax.ppermute(value, inner, [(i, i ^ flip) for i in range(4)])

    block_rows = 16 * rows
    blocks = [along(kv0, flip) for flip in FLIPS]
    dq_shape = jax.ShapeDtypeStruct((2, 2, QR, HD), f32)
    part_shape = jax.ShapeDtypeStruct((block_rows, 4 * HD), bf16)
    options = dict(compiler_params=PARAMS)
    dq, grads, far = pl.pallas_call(
        first_kernel,
        out_shape=(dq_shape, jax.ShapeDtypeStruct((2, R, 4 * HD), bf16), part_shape),
        in_specs=[VMEM] * 3,
        out_specs=(VMEM,) * 3,
        cost_estimate=cost(R + block_rows),
        name="own_keys_and_far_block",
        **options,
    )(mine, recv, blocks[0])
    far = along(far, FLIPS[0])
    dq, near_a, near_b = pl.pallas_call(
        middle_kernel,
        out_shape=(dq_shape, part_shape, part_shape),
        in_specs=[VMEM] * 5,
        out_specs=(VMEM,) * 3,
        input_output_aliases={4: 0},
        cost_estimate=cost(2 * block_rows),
        name="near_blocks",
        **options,
    )(mine, recv, blocks[1], blocks[2], dq)
    near_a = along(near_a, FLIPS[1])
    near_b = along(near_b, FLIPS[2])
    narrow = jax.ShapeDtypeStruct((R, KVH * HD), bf16)
    back, part0, full_dq, full_dk, full_dv = pl.pallas_call(
        last_kernel,
        out_shape=(
            jax.ShapeDtypeStruct((R, 2 * QR + 4 * HD), bf16),
            jax.ShapeDtypeStruct((block_rows, 4 * HD), f32),
            jax.ShapeDtypeStruct((R, H * HD), bf16),
            narrow,
            narrow,
        ),
        in_specs=[SMEM] + [VMEM] * 5 + [ANY],
        out_specs=(VMEM, VMEM, ANY, ANY, ANY),
        scratch_shapes=[pltpu.VMEM((R, 2 * QR), bf16), pltpu.SemaphoreType.DMA((3,))],
        cost_estimate=cost(block_rows),
        name="own_block",
        **options,
    )(core[None], mine, recv, kv0, dq, grads, far)
    total, back = simple(
        sum_blocks_kernel,
        (part_shape, jax.ShapeDtypeStruct(back.shape, bf16)),
        "sum_blocks",
        part0,
        near_a,
        near_b,
        far,
        back,
        in_specs=[VMEM] * 4 + [ANY],
        out_specs=(VMEM, ANY),
        input_output_aliases={4: 1},
    )
    got = lax.ppermute(back, "core", [(0, 1), (1, 0)])
    total = lax.all_to_all(total, outer, 0, 0, tiled=True)
    total = simple(
        sum_copies_kernel, jax.ShapeDtypeStruct((8 * rows, 4 * HD), bf16), "sum_copies", total
    )
    total = lax.all_to_all(total, ("yh", "core"), 0, 0, tiled=True)
    final = jax.ShapeDtypeStruct((rows, KVH * HD), f32)
    prompt_dk, prompt_dv = simple(sum_samples_kernel, (final, final), "sum_samples", total)
    resp_dq, resp_dk, resp_dv = simple(
        join_kernel,
        (jax.ShapeDtypeStruct((R, H * HD), bf16), narrow, narrow),
        "join",
        core[None],
        got,
        full_dq,
        full_dk,
        full_dv,
        in_specs=[SMEM] + [ANY] * 4,
        out_specs=(ANY,) * 3,
        scratch_shapes=[pltpu.SemaphoreType.DMA((3,))],
        input_output_aliases={2: 0, 3: 1, 4: 2},
    )
    return resp_dq[None], resp_dk[None], resp_dv[None], prompt_dk, prompt_dv


def solution(mesh):
    fine = Mesh(mesh.devices.reshape(4, 2, 4, 2, 4, 2), AXES)
    both = P(AXES, None, None)
    prefix = P(("x", "yl", "zh", "zl"), None)
    return jax.shard_map(
        body,
        mesh=fine,
        in_specs=(both,) * 6 + (prefix, prefix, P(AXES)),
        out_specs=(both, both, both, prefix, prefix),
        check_vma=False,
    )
```

```python
import functools
import math

import jax
import jax.numpy as jnp
from jax import lax
from jax.experimental import pallas as pl
from jax.experimental.pallas import tpu as pltpu
from jax.sharding import Mesh
from jax.sharding import PartitionSpec as P

H = 32
KVH = 4
HD = 128
R = 128
G = H // KVH
QR = G * R
SCALE = HD**-0.5
LOG2E = math.log2(math.e)
AXES = ("yh", "core", "x", "yl", "zh", "zl")
f32 = jnp.float32
bf16 = jnp.bfloat16

OFF_DO = QR
OFF_K = 2 * QR
OFF_V = OFF_K + R
OFF_ST = OFF_V + R
PACK = OFF_ST + 6 * G

NT = (((1,), (1,)), ((), ()))
NN = (((1,), (0,)), ((), ()))
VMEM = pl.BlockSpec(memory_space=pltpu.VMEM)
SMEM = pl.BlockSpec(memory_space=pltpu.SMEM)
ANY = pl.BlockSpec(memory_space=pl.ANY)
CHUNK = 512


def dot(a, b, dims):
    return lax.dot_general(a, b, dims, preferred_element_type=f32)


def split3(value):
    hi = value.astype(bf16)
    rest = value - hi.astype(f32)
    mid = rest.astype(bf16)
    low = (rest - mid.astype(f32)).astype(bf16)
    return hi, mid, low


def prep_kernel(info, q, do, out, k, v, lse, order_by, send, mine, q_buf, do_buf, out_buf, k_buf, v_buf, sems, kv_sems):
    core = info[0]
    length = info[1]
    order = (2 * (1 - core), 2 * (1 - core) + 1, 2 * core, 2 * core + 1)
    wide = [
        [
            pltpu.make_async_copy(src.at[:, pl.ds(pl.multiple_of(g * QR, QR), QR)], buf.at[i], sems.at[j, i])
            for j, (src, buf) in enumerate(((q, q_buf), (do, do_buf), (out, out_buf)))
        ]
        for i, g in enumerate(order)
    ]
    narrow = [pltpu.make_async_copy(k, k_buf, kv_sems.at[0]), pltpu.make_async_copy(v, v_buf, kv_sems.at[1])]
    for copies in [narrow] + wide:
        for copy in copies:
            copy.start()
    for copy in narrow:
        copy.wait()
    ones = jnp.ones((8, HD), bf16)
    token = lax.broadcasted_iota(jnp.int32, (G, R), 1)
    for i, g in enumerate(order):
        ref = send if i < 2 else mine
        s = i % 2
        for copy in wide[i]:
            copy.wait()
        rows = []
        for h in range(G):
            cols = slice(h * HD, (h + 1) * HD)
            ref[s, h * R : (h + 1) * R, :] = q_buf[i, :, cols]
            dh = do_buf[i, :, cols]
            ref[s, OFF_DO + h * R : OFF_DO + (h + 1) * R, :] = dh
            prod = dh.astype(f32) * out_buf[i, :, cols].astype(f32)
            hi = prod.astype(bf16)
            low = (prod - hi.astype(f32)).astype(bf16)
            rows.append((dot(ones, hi, NT) + dot(ones, low, NT))[0:1, :])
        head = pl.ds(pl.multiple_of(g * HD, HD), HD)
        ref[s, OFF_K : OFF_K + R, :] = k_buf[:, head]
        ref[s, OFF_V : OFF_V + R, :] = v_buf[:, head]
        delta = jnp.concatenate(rows, 0)
        lse_g = lse[pl.ds(pl.multiple_of(g * G, G), G), :]
        lse2 = jnp.where(token < length, lse_g * LOG2E, 1e30)
        ref[s, OFF_ST:PACK, :] = jnp.concatenate(split3(lse2) + split3(delta), 0)


def prep(core, length, q, do, out, k, v, lse_t, order_by):
    shape = jax.ShapeDtypeStruct((2, PACK, HD), bf16)
    whole = pl.BlockSpec(memory_space=pl.ANY)
    wide = pltpu.VMEM((4, R, QR), bf16)
    narrow = pltpu.VMEM((R, KVH * HD), bf16)
    return pl.pallas_call(
        prep_kernel,
        out_shape=(shape, shape),
        in_specs=[pl.BlockSpec(memory_space=pltpu.SMEM)] + [whole] * 5 + [VMEM, whole],
        out_specs=(VMEM, VMEM),
        scratch_shapes=[wide, wide, wide, narrow, narrow, pltpu.SemaphoreType.DMA((3, 4)), pltpu.SemaphoreType.DMA((2,))],
        compiler_params=pltpu.CompilerParams(vmem_limit_bytes=61 * 2**20),
        cost_estimate=pl.CostEstimate(flops=10**7, bytes_accessed=8 * 2**20, transcendentals=0),
        name="prep",
    )(jnp.stack([core, length]), q, do, out, k, v, lse_t, order_by)


def stat_row(ref, g, kind, first, count):
    base = OFF_ST + kind * 3 * G
    block = [ref[g, base + term * G : base + (term + 1) * G, :].astype(f32) for term in range(3)]
    total = block[0] + block[1] + block[2]
    return jnp.concatenate([total[h : h + 1, :] for h in range(first, first + count)], 1)


def tile_grads(ref, g, chunk, keys, values, causal):
    cs = slice(chunk * CHUNK, (chunk + 1) * CHUNK)
    qc = ref[g, cs, :]
    dc = ref[g, OFF_DO + chunk * CHUNK : OFF_DO + (chunk + 1) * CHUNK, :]
    heads = CHUNK // R
    lse2 = stat_row(ref, g, 0, chunk * heads, heads)
    delta = stat_row(ref, g, 1, chunk * heads, heads)
    scores = dot(keys, qc, NT)
    prob_grad = dot(values, dc, NT)
    probs = jnp.exp2(scores * (SCALE * LOG2E) - lse2)
    if causal:
        shape = scores.shape
        token = lax.broadcasted_iota(jnp.int32, shape, 1) % R
        probs = jnp.where(lax.broadcasted_iota(jnp.int32, shape, 0) <= token, probs, 0.0)
    score_low = (probs * (prob_grad - delta)).astype(bf16)
    dv = dot(probs.astype(bf16), dc, NN)
    dk = dot(score_low, qc, NN)
    dq = lax.dot_general(keys, score_low, (((0,), (0,)), ((), ())), preferred_element_type=f32).T
    return dk, dv, dq, cs


def prompt_block(mine, recv, kv, emit_dq, out):
    rows = kv.shape[0]
    for g in range(2):
        keys = kv[:, g * HD : (g + 1) * HD]
        values = kv[:, (2 + g) * HD : (3 + g) * HD]
        dk = jnp.zeros((rows, HD), f32)
        dv = jnp.zeros((rows, HD), f32)
        for r, ref in enumerate((mine, recv)):
            for chunk in range(QR // CHUNK):
                dk_c, dv_c, dq_c, cs = tile_grads(ref, g, chunk, keys, values, False)
                dk += dk_c
                dv += dv_c
                emit_dq(r, g, cs, dq_c)
        out[:, g * HD : (g + 1) * HD] = (dk * SCALE).astype(out.dtype)
        out[:, (2 + g) * HD : (3 + g) * HD] = dv.astype(out.dtype)


def first_kernel(mine, recv, kv, dq, out):
    def emit_dq(r, g, cs, value):
        dq[r, g, cs, :] = value

    prompt_block(mine, recv, kv, emit_dq, out)


def middle_kernel(count, mine, recv, *refs):
    kvs, dq_in, dq, outs = refs[:count], refs[count], refs[count + 1], refs[count + 2 :]
    for i, (kv, out) in enumerate(zip(kvs, outs)):

        def emit_dq(r, g, cs, value):
            source = dq if i else dq_in
            dq[r, g, cs, :] = source[r, g, cs, :] + value

        prompt_block(mine, recv, kv, emit_dq, out)


def last_kernel(core, mine, recv, dq_in, order_by, back, full_dq, full_dk, full_dv, own, grads, sems):
    half = 2 * HD

    def place(full, width):
        return full.at[:, pl.ds(pl.multiple_of(core[0] * width, width), width)]

    copies = [
        pltpu.make_async_copy(own, place(full_dq, 2 * QR), sems.at[0]),
        pltpu.make_async_copy(grads.at[:, :half], place(full_dk, half), sems.at[1]),
        pltpu.make_async_copy(grads.at[:, half:], place(full_dv, half), sems.at[2]),
    ]
    for r, (ref, target) in enumerate(((mine, own), (recv, back))):
        dest, base = (grads, 0) if r == 0 else (back, 2 * QR)
        for g in range(2):
            keys = ref[g, OFF_K : OFF_K + R, :]
            values = ref[g, OFF_V : OFF_V + R, :]
            dk = jnp.zeros((R, HD), f32)
            dv = jnp.zeros((R, HD), f32)
            for chunk in range(QR // CHUNK):
                dk_c, dv_c, dq_c, cs = tile_grads(ref, g, chunk, keys, values, True)
                dk += dk_c
                dv += dv_c
                total = ((dq_in[r, g, cs, :] + dq_c) * SCALE).astype(bf16)
                for j in range(CHUNK // R):
                    h = g * G + chunk * (CHUNK // R) + j
                    target[:, h * HD : (h + 1) * HD] = total[j * R : (j + 1) * R, :]
            dest[:, base + g * HD : base + (g + 1) * HD] = (dk * SCALE).astype(bf16)
            dest[:, base + (2 + g) * HD : base + (3 + g) * HD] = dv.astype(bf16)
        if r == 0:
            for copy in copies:
                copy.start()
    for copy in copies:
        copy.wait()


def join_kernel(core, got, in_dq, in_dk, in_dv, full_dq, full_dk, full_dv, sems):
    half = 2 * HD
    other = 1 - core[0]
    copies = []
    for i, (full, start, width) in enumerate(
        ((full_dq, 0, 2 * QR), (full_dk, 2 * QR, half), (full_dv, 2 * QR + half, half))
    ):
        place = full.at[:, pl.ds(pl.multiple_of(other * width, width), width)]
        copies.append(pltpu.make_async_copy(got.at[:, start : start + width], place, sems.at[i]))
    for copy in copies:
        copy.start()
    for copy in copies:
        copy.wait()


def same_kernel(x, y, o, p):
    pass


def shard_kernel(core, k, v, o):
    rows = k.shape[0]
    cols = pl.ds(pl.multiple_of(core[0] * 2 * HD, 2 * HD), 2 * HD)
    shard = jnp.concatenate([k[:, cols], v[:, cols]], 1)
    for i in range(o.shape[0] // rows):
        o[i * rows : (i + 1) * rows, :] = shard


def sum_blocks_kernel(a, b, c, d, back_in, o, back):
    o[...] = (a[...] + b[...].astype(f32) + c[...].astype(f32) + d[...].astype(f32)).astype(bf16)


def sum_copies_kernel(x, o):
    rows = 16
    total = x[0:rows, :].astype(f32)
    for i in range(1, x.shape[0] // rows):
        total += x[i * rows : (i + 1) * rows, :].astype(f32)
    total = total.astype(bf16)
    for i in range(o.shape[0] // rows):
        o[i * rows : (i + 1) * rows, :] = total


def sum_samples_kernel(x, dk, dv):
    rows = 16
    half = 2 * HD
    for c in range(2):
        total = x[c * rows : (c + 1) * rows, :].astype(f32)
        for y in range(1, 4):
            at = (2 * y + c) * rows
            total += x[at : at + rows, :].astype(f32)
        dk[:, c * half : (c + 1) * half] = total[:, :half]
        dv[:, c * half : (c + 1) * half] = total[:, half:]


def simple(kernel, out_shape, name, *args, in_specs=None, out_specs=None, limit=16, **options):
    single = not isinstance(out_shape, tuple)
    return pl.pallas_call(
        kernel,
        out_shape=out_shape,
        in_specs=in_specs or [VMEM] * len(args),
        out_specs=out_specs or (VMEM if single else (VMEM,) * len(out_shape)),
        compiler_params=pltpu.CompilerParams(vmem_limit_bytes=int(limit * 2**20)),
        name=name,
        **options,
    )(*args)


def cost(rows):
    return pl.CostEstimate(
        flops=5 * 2 * rows * 4 * QR * HD, bytes_accessed=8 * 2**20, transcendentals=rows * 4 * QR
    )


PARAMS = pltpu.CompilerParams(vmem_limit_bytes=24 * 2**20)


def body(resp_q, resp_k, resp_v, resp_do, resp_out, resp_lse, prompt_k, prompt_v, resp_lengths):
    core = lax.axis_index("core").astype(jnp.int32)
    rows = prompt_k.shape[0]
    outer = ("yl", "zh", "zl")
    inner = "x"

    shards = simple(
        shard_kernel,
        jax.ShapeDtypeStruct((16 * rows, 4 * HD), bf16),
        "shards",
        core[None],
        prompt_k,
        prompt_v,
        in_specs=[SMEM, VMEM, VMEM],
        limit=61,
    )
    kv0 = lax.all_to_all(shards, outer, 0, 0, tiled=True)
    send, mine = prep(
        core,
        resp_lengths[0],
        resp_q[0],
        resp_do[0],
        resp_out[0],
        resp_k[0],
        resp_v[0],
        resp_lse[0].T,
        shards,
    )
    kv0, send = simple(
        same_kernel,
        (jax.ShapeDtypeStruct(kv0.shape, bf16), jax.ShapeDtypeStruct(send.shape, bf16)),
        "gathered_and_prepared",
        kv0,
        send,
        in_specs=[ANY, ANY],
        out_specs=(ANY, ANY),
        input_output_aliases={0: 0, 1: 1},
        limit=62.25,
    )
    recv = lax.ppermute(send, "core", [(0, 1), (1, 0)])

    def along(value, flip):
        return lax.ppermute(value, inner, [(i, i ^ flip) for i in range(4)])

    block_rows = 16 * rows
    kv_far = along(kv0, 2)
    kv_a = along(kv0, 1)
    kv_b = along(kv0, 3)
    dq_shape = jax.ShapeDtypeStruct((2, 2, QR, HD), f32)
    part_shape = jax.ShapeDtypeStruct((block_rows, 4 * HD), bf16)
    options = dict(compiler_params=PARAMS)
    dq, part0 = pl.pallas_call(
        first_kernel,
        out_shape=(dq_shape, jax.ShapeDtypeStruct((block_rows, 4 * HD), f32)),
        in_specs=[VMEM] * 3,
        out_specs=(VMEM,) * 2,
        cost_estimate=cost(block_rows),
        name="own_block",
        **options,
    )(mine, recv, kv0)

    def middle(kvs, dq):
        count = len(kvs)
        return pl.pallas_call(
            functools.partial(middle_kernel, count),
            out_shape=(dq_shape,) + (part_shape,) * count,
            in_specs=[VMEM] * (3 + count),
            out_specs=(VMEM,) * (1 + count),
            input_output_aliases={2 + count: 0},
            cost_estimate=cost(count * block_rows),
            name="other_blocks",
            **options,
        )(mine, recv, *kvs, dq)

    dq, far = middle([kv_far], dq)
    far = along(far, 2)
    dq, near_a, near_b = middle([kv_a, kv_b], dq)
    near_a = along(near_a, 1)
    near_b = along(near_b, 3)
    narrow = jax.ShapeDtypeStruct((R, KVH * HD), bf16)
    back, full_dq, full_dk, full_dv = pl.pallas_call(
        last_kernel,
        out_shape=(
            jax.ShapeDtypeStruct((R, 2 * QR + 4 * HD), bf16),
            jax.ShapeDtypeStruct((R, H * HD), bf16),
            narrow,
            narrow,
        ),
        in_specs=[SMEM] + [VMEM] * 3 + [ANY],
        out_specs=(VMEM, ANY, ANY, ANY),
        scratch_shapes=[
            pltpu.VMEM((R, 2 * QR), bf16),
            pltpu.VMEM((R, 4 * HD), bf16),
            pltpu.SemaphoreType.DMA((3,)),
        ],
        cost_estimate=cost(R),
        name="own_keys",
        **options,
    )(core[None], mine, recv, dq, far)
    total, back = simple(
        sum_blocks_kernel,
        (part_shape, jax.ShapeDtypeStruct(back.shape, bf16)),
        "sum_blocks",
        part0,
        near_a,
        near_b,
        far,
        back,
        in_specs=[VMEM] * 4 + [ANY],
        out_specs=(VMEM, ANY),
        input_output_aliases={4: 1},
    )
    got = lax.ppermute(back, "core", [(0, 1), (1, 0)])
    total = lax.all_to_all(total, outer, 0, 0, tiled=True)
    total = simple(
        sum_copies_kernel, jax.ShapeDtypeStruct((8 * rows, 4 * HD), bf16), "sum_copies", total
    )
    total = lax.all_to_all(total, ("yh", "core"), 0, 0, tiled=True)
    final = jax.ShapeDtypeStruct((rows, KVH * HD), f32)
    prompt_dk, prompt_dv = simple(sum_samples_kernel, (final, final), "sum_samples", total)
    resp_dq, resp_dk, resp_dv = simple(
        join_kernel,
        (jax.ShapeDtypeStruct((R, H * HD), bf16), narrow, narrow),
        "join",
        core[None],
        got,
        full_dq,
        full_dk,
        full_dv,
        in_specs=[SMEM] + [ANY] * 4,
        out_specs=(ANY,) * 3,
        scratch_shapes=[pltpu.SemaphoreType.DMA((3,))],
        input_output_aliases={2: 0, 3: 1, 4: 2},
    )
    return resp_dq[None], resp_dk[None], resp_dv[None], prompt_dk, prompt_dv


def solution(mesh):
    fine = Mesh(mesh.devices.reshape(4, 2, 4, 2, 4, 2), AXES)
    both = P(AXES, None, None)
    prefix = P(("x", "yl", "zh", "zl"), None)
    return jax.shard_map(
        body,
        mesh=fine,
        in_specs=(both,) * 6 + (prefix, prefix, P(AXES)),
        out_specs=(both, both, both, prefix, prefix),
        check_vma=False,
    )
```

```python
import functools
import math

import jax
import jax.numpy as jnp
from jax import lax
from jax.experimental import pallas as pl
from jax.experimental.pallas import tpu as pltpu
from jax.sharding import Mesh
from jax.sharding import PartitionSpec as P

H = 32
KVH = 4
HD = 128
R = 128
G = H // KVH
QR = G * R
SCALE = HD**-0.5
LOG2E = math.log2(math.e)
AXES = ("yh", "core", "x", "yl", "zh", "zl")
f32 = jnp.float32
bf16 = jnp.bfloat16

OFF_DO = QR
OFF_K = 2 * QR
OFF_V = OFF_K + R
OFF_ST = OFF_V + R
PACK = OFF_ST + 6 * G

NT = (((1,), (1,)), ((), ()))
NN = (((1,), (0,)), ((), ()))
VMEM = pl.BlockSpec(memory_space=pltpu.VMEM)
SMEM = pl.BlockSpec(memory_space=pltpu.SMEM)
ANY = pl.BlockSpec(memory_space=pl.ANY)
FLIPS = (2, 1, 3)
CHUNK = 512


def dot(a, b, dims):
    return lax.dot_general(a, b, dims, preferred_element_type=f32)


def split3(value):
    hi = value.astype(bf16)
    rest = value - hi.astype(f32)
    mid = rest.astype(bf16)
    low = (rest - mid.astype(f32)).astype(bf16)
    return hi, mid, low


def prep_kernel(info, q, do, out, k, v, lse, order_by, send, mine, q_buf, do_buf, out_buf, k_buf, v_buf, sems, kv_sems):
    core = info[0]
    length = info[1]
    order = (2 * (1 - core), 2 * (1 - core) + 1, 2 * core, 2 * core + 1)
    wide = [
        [
            pltpu.make_async_copy(src.at[:, pl.ds(pl.multiple_of(g * QR, QR), QR)], buf.at[i], sems.at[j, i])
            for j, (src, buf) in enumerate(((q, q_buf), (do, do_buf), (out, out_buf)))
        ]
        for i, g in enumerate(order)
    ]
    narrow = [pltpu.make_async_copy(k, k_buf, kv_sems.at[0]), pltpu.make_async_copy(v, v_buf, kv_sems.at[1])]
    for copies in [narrow] + wide:
        for copy in copies:
            copy.start()
    for copy in narrow:
        copy.wait()
    ones = jnp.ones((8, HD), bf16)
    token = lax.broadcasted_iota(jnp.int32, (G, R), 1)
    for i, g in enumerate(order):
        ref = send if i < 2 else mine
        s = i % 2
        for copy in wide[i]:
            copy.wait()
        rows = []
        for h in range(G):
            cols = slice(h * HD, (h + 1) * HD)
            ref[s, h * R : (h + 1) * R, :] = q_buf[i, :, cols]
            dh = do_buf[i, :, cols]
            ref[s, OFF_DO + h * R : OFF_DO + (h + 1) * R, :] = dh
            prod = dh.astype(f32) * out_buf[i, :, cols].astype(f32)
            hi = prod.astype(bf16)
            low = (prod - hi.astype(f32)).astype(bf16)
            rows.append((dot(ones, hi, NT) + dot(ones, low, NT))[0:1, :])
        head = pl.ds(pl.multiple_of(g * HD, HD), HD)
        ref[s, OFF_K : OFF_K + R, :] = k_buf[:, head]
        ref[s, OFF_V : OFF_V + R, :] = v_buf[:, head]
        delta = jnp.concatenate(rows, 0)
        lse_g = lse[pl.ds(pl.multiple_of(g * G, G), G), :]
        lse2 = jnp.where(token < length, lse_g * LOG2E, 1e30)
        ref[s, OFF_ST:PACK, :] = jnp.concatenate(split3(lse2) + split3(delta), 0)


def prep(core, length, q, do, out, k, v, lse_t, order_by):
    shape = jax.ShapeDtypeStruct((2, PACK, HD), bf16)
    whole = pl.BlockSpec(memory_space=pl.ANY)
    wide = pltpu.VMEM((4, R, QR), bf16)
    narrow = pltpu.VMEM((R, KVH * HD), bf16)
    return pl.pallas_call(
        prep_kernel,
        out_shape=(shape, shape),
        in_specs=[pl.BlockSpec(memory_space=pltpu.SMEM)] + [whole] * 5 + [VMEM, whole],
        out_specs=(VMEM, VMEM),
        scratch_shapes=[wide, wide, wide, narrow, narrow, pltpu.SemaphoreType.DMA((3, 4)), pltpu.SemaphoreType.DMA((2,))],
        compiler_params=pltpu.CompilerParams(vmem_limit_bytes=61 * 2**20),
        cost_estimate=pl.CostEstimate(flops=10**7, bytes_accessed=8 * 2**20, transcendentals=0),
        name="prep",
    )(jnp.stack([core, length]), q, do, out, k, v, lse_t, order_by)


def stat_row(ref, g, kind, first, count):
    base = OFF_ST + kind * 3 * G
    block = [ref[g, base + term * G : base + (term + 1) * G, :].astype(f32) for term in range(3)]
    total = block[0] + block[1] + block[2]
    return jnp.concatenate([total[h : h + 1, :] for h in range(first, first + count)], 1)


def tile_grads(ref, g, chunk, keys, values, causal):
    cs = slice(chunk * CHUNK, (chunk + 1) * CHUNK)
    qc = ref[g, cs, :]
    dc = ref[g, OFF_DO + chunk * CHUNK : OFF_DO + (chunk + 1) * CHUNK, :]
    heads = CHUNK // R
    lse2 = stat_row(ref, g, 0, chunk * heads, heads)
    delta = stat_row(ref, g, 1, chunk * heads, heads)
    scores = dot(keys, qc, NT)
    prob_grad = dot(values, dc, NT)
    probs = jnp.exp2(scores * (SCALE * LOG2E) - lse2)
    if causal:
        shape = scores.shape
        token = lax.broadcasted_iota(jnp.int32, shape, 1) % R
        probs = jnp.where(lax.broadcasted_iota(jnp.int32, shape, 0) <= token, probs, 0.0)
    score_low = (probs * (prob_grad - delta)).astype(bf16)
    dv = dot(probs.astype(bf16), dc, NN)
    dk = dot(score_low, qc, NN)
    dq = lax.dot_general(keys, score_low, (((0,), (0,)), ((), ())), preferred_element_type=f32).T
    return dk, dv, dq, cs


def prompt_block(mine, recv, kv, emit_dq, out):
    rows = kv.shape[0]
    for g in range(2):
        keys = kv[:, g * HD : (g + 1) * HD]
        values = kv[:, (2 + g) * HD : (3 + g) * HD]
        dk = jnp.zeros((rows, HD), f32)
        dv = jnp.zeros((rows, HD), f32)
        for r, ref in enumerate((mine, recv)):
            for chunk in range(QR // CHUNK):
                dk_c, dv_c, dq_c, cs = tile_grads(ref, g, chunk, keys, values, False)
                dk += dk_c
                dv += dv_c
                emit_dq(r, g, cs, dq_c)
        out[:, g * HD : (g + 1) * HD] = (dk * SCALE).astype(out.dtype)
        out[:, (2 + g) * HD : (3 + g) * HD] = dv.astype(out.dtype)


def first_kernel(mine, recv, kv, dq, out):
    def emit_dq(r, g, cs, value):
        dq[r, g, cs, :] = value

    prompt_block(mine, recv, kv, emit_dq, out)


def middle_kernel(mine, recv, kv_a, kv_b, dq_in, dq, out_a, out_b):
    def emit_a(r, g, cs, value):
        dq[r, g, cs, :] = dq_in[r, g, cs, :] + value

    def emit_b(r, g, cs, value):
        dq[r, g, cs, :] += value

    prompt_block(mine, recv, kv_a, emit_a, out_a)
    prompt_block(mine, recv, kv_b, emit_b, out_b)


def last_kernel(core, mine, recv, kv, dq_in, order_by, back, out, full_dq, full_dk, full_dv, dq, own, grads, sems):
    half = 2 * HD

    def emit_block(r, g, cs, value):
        dq[r, g, cs, :] = dq_in[r, g, cs, :] + value

    def place(full, width):
        return full.at[:, pl.ds(pl.multiple_of(core[0] * width, width), width)]

    copies = [
        pltpu.make_async_copy(own, place(full_dq, 2 * QR), sems.at[0]),
        pltpu.make_async_copy(grads.at[:, :half], place(full_dk, half), sems.at[1]),
        pltpu.make_async_copy(grads.at[:, half:], place(full_dv, half), sems.at[2]),
    ]
    prompt_block(mine, recv, kv, emit_block, out)
    for r, (ref, target) in enumerate(((mine, own), (recv, back))):
        dest, base = (grads, 0) if r == 0 else (back, 2 * QR)
        for g in range(2):
            keys = ref[g, OFF_K : OFF_K + R, :]
            values = ref[g, OFF_V : OFF_V + R, :]
            dk = jnp.zeros((R, HD), f32)
            dv = jnp.zeros((R, HD), f32)
            for chunk in range(QR // CHUNK):
                dk_c, dv_c, dq_c, cs = tile_grads(ref, g, chunk, keys, values, True)
                dk += dk_c
                dv += dv_c
                total = ((dq[r, g, cs, :] + dq_c) * SCALE).astype(bf16)
                for j in range(CHUNK // R):
                    h = g * G + chunk * (CHUNK // R) + j
                    target[:, h * HD : (h + 1) * HD] = total[j * R : (j + 1) * R, :]
            dest[:, base + g * HD : base + (g + 1) * HD] = (dk * SCALE).astype(bf16)
            dest[:, base + (2 + g) * HD : base + (3 + g) * HD] = dv.astype(bf16)
        if r == 0:
            for copy in copies:
                copy.start()
    for copy in copies:
        copy.wait()


def join_kernel(core, got, in_dq, in_dk, in_dv, full_dq, full_dk, full_dv, sems):
    half = 2 * HD
    other = 1 - core[0]
    copies = []
    for i, (full, start, width) in enumerate(
        ((full_dq, 0, 2 * QR), (full_dk, 2 * QR, half), (full_dv, 2 * QR + half, half))
    ):
        place = full.at[:, pl.ds(pl.multiple_of(other * width, width), width)]
        copies.append(pltpu.make_async_copy(got.at[:, start : start + width], place, sems.at[i]))
    for copy in copies:
        copy.start()
    for copy in copies:
        copy.wait()


def same_kernel(x, y, o, p):
    pass


def shard_kernel(core, k, v, o):
    rows = k.shape[0]
    cols = pl.ds(pl.multiple_of(core[0] * 2 * HD, 2 * HD), 2 * HD)
    shard = jnp.concatenate([k[:, cols], v[:, cols]], 1)
    for i in range(o.shape[0] // rows):
        o[i * rows : (i + 1) * rows, :] = shard


def sum_blocks_kernel(a, b, c, d, back_in, o, back):
    o[...] = (a[...] + b[...].astype(f32) + c[...].astype(f32) + d[...].astype(f32)).astype(bf16)


def sum_copies_kernel(x, o):
    rows = 16
    total = x[0:rows, :].astype(f32)
    for i in range(1, x.shape[0] // rows):
        total += x[i * rows : (i + 1) * rows, :].astype(f32)
    total = total.astype(bf16)
    for i in range(o.shape[0] // rows):
        o[i * rows : (i + 1) * rows, :] = total


def sum_samples_kernel(x, dk, dv):
    rows = 16
    half = 2 * HD
    for c in range(2):
        total = x[c * rows : (c + 1) * rows, :].astype(f32)
        for y in range(1, 4):
            at = (2 * y + c) * rows
            total += x[at : at + rows, :].astype(f32)
        dk[:, c * half : (c + 1) * half] = total[:, :half]
        dv[:, c * half : (c + 1) * half] = total[:, half:]


def simple(kernel, out_shape, name, *args, in_specs=None, out_specs=None, limit=16, **options):
    single = not isinstance(out_shape, tuple)
    return pl.pallas_call(
        kernel,
        out_shape=out_shape,
        in_specs=in_specs or [VMEM] * len(args),
        out_specs=out_specs or (VMEM if single else (VMEM,) * len(out_shape)),
        compiler_params=pltpu.CompilerParams(vmem_limit_bytes=int(limit * 2**20)),
        name=name,
        **options,
    )(*args)


def cost(rows):
    return pl.CostEstimate(
        flops=5 * 2 * rows * 4 * QR * HD, bytes_accessed=8 * 2**20, transcendentals=rows * 4 * QR
    )


PARAMS = pltpu.CompilerParams(vmem_limit_bytes=24 * 2**20)


def body(resp_q, resp_k, resp_v, resp_do, resp_out, resp_lse, prompt_k, prompt_v, resp_lengths):
    core = lax.axis_index("core").astype(jnp.int32)
    rows = prompt_k.shape[0]
    outer = ("yl", "zh", "zl")
    inner = "x"

    shards = simple(
        shard_kernel,
        jax.ShapeDtypeStruct((16 * rows, 4 * HD), bf16),
        "shards",
        core[None],
        prompt_k,
        prompt_v,
        in_specs=[SMEM, VMEM, VMEM],
        limit=61,
    )
    kv0 = lax.all_to_all(shards, outer, 0, 0, tiled=True)
    send, mine = prep(
        core,
        resp_lengths[0],
        resp_q[0],
        resp_do[0],
        resp_out[0],
        resp_k[0],
        resp_v[0],
        resp_lse[0].T,
        shards,
    )
    kv0, send = simple(
        same_kernel,
        (jax.ShapeDtypeStruct(kv0.shape, bf16), jax.ShapeDtypeStruct(send.shape, bf16)),
        "gathered_and_prepared",
        kv0,
        send,
        in_specs=[ANY, ANY],
        out_specs=(ANY, ANY),
        input_output_aliases={0: 0, 1: 1},
        limit=62.25,
    )
    recv = lax.ppermute(send, "core", [(0, 1), (1, 0)])

    def along(value, flip):
        return lax.ppermute(value, inner, [(i, i ^ flip) for i in range(4)])

    block_rows = 16 * rows
    blocks = [along(kv0, flip) for flip in FLIPS]
    dq_shape = jax.ShapeDtypeStruct((2, 2, QR, HD), f32)
    part_shape = jax.ShapeDtypeStruct((block_rows, 4 * HD), bf16)
    options = dict(compiler_params=PARAMS)
    dq, part1 = pl.pallas_call(
        first_kernel,
        out_shape=(dq_shape, part_shape),
        in_specs=[VMEM] * 3,
        out_specs=(VMEM,) * 2,
        cost_estimate=cost(block_rows),
        name="far_block",
        **options,
    )(mine, recv, blocks[0])
    part1 = along(part1, FLIPS[0])
    dq, part2, part3 = pl.pallas_call(
        middle_kernel,
        out_shape=(dq_shape, part_shape, part_shape),
        in_specs=[VMEM] * 5,
        out_specs=(VMEM,) * 3,
        input_output_aliases={4: 0},
        cost_estimate=cost(2 * block_rows),
        name="near_blocks",
        **options,
    )(mine, recv, blocks[1], blocks[2], dq)
    part2 = along(part2, FLIPS[1])
    part3 = along(part3, FLIPS[2])
    narrow = jax.ShapeDtypeStruct((R, KVH * HD), bf16)
    back, part0, full_dq, full_dk, full_dv = pl.pallas_call(
        last_kernel,
        out_shape=(
            jax.ShapeDtypeStruct((R, 2 * QR + 4 * HD), bf16),
            jax.ShapeDtypeStruct((block_rows, 4 * HD), f32),
            jax.ShapeDtypeStruct((R, H * HD), bf16),
            narrow,
            narrow,
        ),
        in_specs=[SMEM] + [VMEM] * 4 + [ANY],
        out_specs=(VMEM, VMEM, ANY, ANY, ANY),
        scratch_shapes=[
            pltpu.VMEM((2, 2, QR, HD), f32),
            pltpu.VMEM((R, 2 * QR), bf16),
            pltpu.VMEM((R, 4 * HD), bf16),
            pltpu.SemaphoreType.DMA((3,)),
        ],
        cost_estimate=cost(block_rows + R),
        name="own_block_and_own_keys",
        **options,
    )(core[None], mine, recv, kv0, dq, part1)
    total, back = simple(
        sum_blocks_kernel,
        (part_shape, jax.ShapeDtypeStruct(back.shape, bf16)),
        "sum_blocks",
        part0,
        part1,
        part3,
        part2,
        back,
        in_specs=[VMEM] * 4 + [ANY],
        out_specs=(VMEM, ANY),
        input_output_aliases={4: 1},
    )
    got = lax.ppermute(back, "core", [(0, 1), (1, 0)])
    total = lax.all_to_all(total, outer, 0, 0, tiled=True)
    total = simple(
        sum_copies_kernel, jax.ShapeDtypeStruct((8 * rows, 4 * HD), bf16), "sum_copies", total
    )
    total = lax.all_to_all(total, ("yh", "core"), 0, 0, tiled=True)
    final = jax.ShapeDtypeStruct((rows, KVH * HD), f32)
    prompt_dk, prompt_dv = simple(sum_samples_kernel, (final, final), "sum_samples", total)
    resp_dq, resp_dk, resp_dv = simple(
        join_kernel,
        (jax.ShapeDtypeStruct((R, H * HD), bf16), narrow, narrow),
        "join",
        core[None],
        got,
        full_dq,
        full_dk,
        full_dv,
        in_specs=[SMEM] + [ANY] * 4,
        out_specs=(ANY,) * 3,
        scratch_shapes=[pltpu.SemaphoreType.DMA((3,))],
        input_output_aliases={2: 0, 3: 1, 4: 2},
    )
    return resp_dq[None], resp_dk[None], resp_dv[None], prompt_dk, prompt_dv


def solution(mesh):
    fine = Mesh(mesh.devices.reshape(4, 2, 4, 2, 4, 2), AXES)
    both = P(AXES, None, None)
    prefix = P(("x", "yl", "zh", "zl"), None)
    return jax.shard_map(
        body,
        mesh=fine,
        in_specs=(both,) * 6 + (prefix, prefix, P(AXES)),
        out_specs=(both, both, both, prefix, prefix),
        check_vma=False,
    )
```

```python
import functools
import math

import jax
import jax.numpy as jnp
from jax import lax
from jax.experimental import pallas as pl
from jax.experimental.pallas import tpu as pltpu
from jax.sharding import Mesh
from jax.sharding import PartitionSpec as P

H = 32
KVH = 4
HD = 128
R = 128
G = H // KVH
QR = G * R
SCALE = HD**-0.5
LOG2E = math.log2(math.e)
AXES = ("yh", "core", "x", "yl", "zh", "zl")
f32 = jnp.float32
bf16 = jnp.bfloat16

OFF_DO = QR
OFF_K = 2 * QR
OFF_V = OFF_K + R
OFF_ST = OFF_V + R
PACK = OFF_ST + 6 * G

NT = (((1,), (1,)), ((), ()))
NN = (((1,), (0,)), ((), ()))
VMEM = pl.BlockSpec(memory_space=pltpu.VMEM)
SMEM = pl.BlockSpec(memory_space=pltpu.SMEM)
ANY = pl.BlockSpec(memory_space=pl.ANY)
FLIPS = (2, 1, 3)
CHUNK = 512


def dot(a, b, dims):
    return lax.dot_general(a, b, dims, preferred_element_type=f32)


def split3(value):
    hi = value.astype(bf16)
    rest = value - hi.astype(f32)
    mid = rest.astype(bf16)
    low = (rest - mid.astype(f32)).astype(bf16)
    return hi, mid, low


def prep_kernel(core_ref, length_ref, q, do, out, k, v, lse, order_by, send, mine, q_buf, do_buf, out_buf, k_buf, v_buf, sems, kv_sems):
    core = core_ref[0]
    length = length_ref[0]
    order = (2 * (1 - core), 2 * (1 - core) + 1, 2 * core, 2 * core + 1)
    wide = [
        [
            pltpu.make_async_copy(src.at[:, pl.ds(pl.multiple_of(g * QR, QR), QR)], buf.at[i], sems.at[j, i])
            for j, (src, buf) in enumerate(((q, q_buf), (do, do_buf), (out, out_buf)))
        ]
        for i, g in enumerate(order)
    ]
    narrow = [pltpu.make_async_copy(k, k_buf, kv_sems.at[0]), pltpu.make_async_copy(v, v_buf, kv_sems.at[1])]
    for copies in [narrow] + wide:
        for copy in copies:
            copy.start()
    for copy in narrow:
        copy.wait()
    ones = jnp.ones((8, HD), bf16)
    token = lax.broadcasted_iota(jnp.int32, (G, R), 1)
    for i, g in enumerate(order):
        ref = send if i < 2 else mine
        s = i % 2
        for copy in wide[i]:
            copy.wait()
        rows = []
        for h in range(G):
            cols = slice(h * HD, (h + 1) * HD)
            ref[s, h * R : (h + 1) * R, :] = q_buf[i, :, cols]
            dh = do_buf[i, :, cols]
            ref[s, OFF_DO + h * R : OFF_DO + (h + 1) * R, :] = dh
            prod = dh.astype(f32) * out_buf[i, :, cols].astype(f32)
            hi = prod.astype(bf16)
            low = (prod - hi.astype(f32)).astype(bf16)
            rows.append((dot(ones, hi, NT) + dot(ones, low, NT))[0:1, :])
        head = pl.ds(pl.multiple_of(g * HD, HD), HD)
        ref[s, OFF_K : OFF_K + R, :] = k_buf[:, head]
        ref[s, OFF_V : OFF_V + R, :] = v_buf[:, head]
        delta = jnp.concatenate(rows, 0)
        lse_g = lse[pl.ds(pl.multiple_of(g * G, G), G), :]
        lse2 = jnp.where(token < length, lse_g * LOG2E, 1e30)
        ref[s, OFF_ST:PACK, :] = jnp.concatenate(split3(lse2) + split3(delta), 0)


def prep(core, length, q, do, out, k, v, lse_t, order_by):
    shape = jax.ShapeDtypeStruct((2, PACK, HD), bf16)
    whole = pl.BlockSpec(memory_space=pl.ANY)
    wide = pltpu.VMEM((4, R, QR), bf16)
    narrow = pltpu.VMEM((R, KVH * HD), bf16)
    return pl.pallas_call(
        prep_kernel,
        out_shape=(shape, shape),
        in_specs=[SMEM, SMEM] + [whole] * 5 + [VMEM, whole],
        out_specs=(VMEM, VMEM),
        scratch_shapes=[wide, wide, wide, narrow, narrow, pltpu.SemaphoreType.DMA((3, 4)), pltpu.SemaphoreType.DMA((2,))],
        compiler_params=pltpu.CompilerParams(vmem_limit_bytes=61 * 2**20),
        cost_estimate=pl.CostEstimate(flops=10**7, bytes_accessed=8 * 2**20, transcendentals=0),
        name="prep",
    )(core[None], length, q, do, out, k, v, lse_t, order_by)


def stat_row(ref, g, kind, first, count):
    base = OFF_ST + kind * 3 * G
    block = [ref[g, base + term * G : base + (term + 1) * G, :].astype(f32) for term in range(3)]
    total = block[0] + block[1] + block[2]
    return jnp.concatenate([total[h : h + 1, :] for h in range(first, first + count)], 1)


def tile_grads(ref, g, chunk, keys, values, causal):
    cs = slice(chunk * CHUNK, (chunk + 1) * CHUNK)
    qc = ref[g, cs, :]
    dc = ref[g, OFF_DO + chunk * CHUNK : OFF_DO + (chunk + 1) * CHUNK, :]
    heads = CHUNK // R
    lse2 = stat_row(ref, g, 0, chunk * heads, heads)
    delta = stat_row(ref, g, 1, chunk * heads, heads)
    scores = dot(keys, qc, NT)
    prob_grad = dot(values, dc, NT)
    probs = jnp.exp2(scores * (SCALE * LOG2E) - lse2)
    if causal:
        shape = scores.shape
        token = lax.broadcasted_iota(jnp.int32, shape, 1) % R
        probs = jnp.where(lax.broadcasted_iota(jnp.int32, shape, 0) <= token, probs, 0.0)
    score_low = (probs * (prob_grad - delta)).astype(bf16)
    dv = dot(probs.astype(bf16), dc, NN)
    dk = dot(score_low, qc, NN)
    dq = lax.dot_general(keys, score_low, (((0,), (0,)), ((), ())), preferred_element_type=f32).T
    return dk, dv, dq, cs


def prompt_block(mine, recv, kv, emit_dq, out):
    rows = kv.shape[0]
    for g in range(2):
        keys = kv[:, g * HD : (g + 1) * HD]
        values = kv[:, (2 + g) * HD : (3 + g) * HD]
        dk = jnp.zeros((rows, HD), f32)
        dv = jnp.zeros((rows, HD), f32)
        for r, ref in enumerate((mine, recv)):
            for chunk in range(QR // CHUNK):
                dk_c, dv_c, dq_c, cs = tile_grads(ref, g, chunk, keys, values, False)
                dk += dk_c
                dv += dv_c
                emit_dq(r, g, cs, dq_c)
        out[:, g * HD : (g + 1) * HD] = (dk * SCALE).astype(out.dtype)
        out[:, (2 + g) * HD : (3 + g) * HD] = dv.astype(out.dtype)


def first_kernel(mine, recv, kv, dq, out):
    def emit_dq(r, g, cs, value):
        dq[r, g, cs, :] = value

    prompt_block(mine, recv, kv, emit_dq, out)


def middle_kernel(mine, recv, kv_a, kv_b, dq_in, dq, out_a, out_b):
    def emit_a(r, g, cs, value):
        dq[r, g, cs, :] = dq_in[r, g, cs, :] + value

    def emit_b(r, g, cs, value):
        dq[r, g, cs, :] += value

    prompt_block(mine, recv, kv_a, emit_a, out_a)
    prompt_block(mine, recv, kv_b, emit_b, out_b)


def last_kernel(core, mine, recv, kv, dq_in, order_by, back, out, full_dq, full_dk, full_dv, dq, own, grads, sems):
    half = 2 * HD

    def emit_block(r, g, cs, value):
        dq[r, g, cs, :] = dq_in[r, g, cs, :] + value

    def place(full, width):
        return full.at[:, pl.ds(pl.multiple_of(core[0] * width, width), width)]

    copies = [
        pltpu.make_async_copy(own, place(full_dq, 2 * QR), sems.at[0]),
        pltpu.make_async_copy(grads.at[:, :half], place(full_dk, half), sems.at[1]),
        pltpu.make_async_copy(grads.at[:, half:], place(full_dv, half), sems.at[2]),
    ]
    prompt_block(mine, recv, kv, emit_block, out)
    for r, (ref, target) in enumerate(((mine, own), (recv, back))):
        dest, base = (grads, 0) if r == 0 else (back, 2 * QR)
        for g in range(2):
            keys = ref[g, OFF_K : OFF_K + R, :]
            values = ref[g, OFF_V : OFF_V + R, :]
            dk = jnp.zeros((R, HD), f32)
            dv = jnp.zeros((R, HD), f32)
            for chunk in range(QR // CHUNK):
                dk_c, dv_c, dq_c, cs = tile_grads(ref, g, chunk, keys, values, True)
                dk += dk_c
                dv += dv_c
                total = ((dq[r, g, cs, :] + dq_c) * SCALE).astype(bf16)
                for j in range(CHUNK // R):
                    h = g * G + chunk * (CHUNK // R) + j
                    target[:, h * HD : (h + 1) * HD] = total[j * R : (j + 1) * R, :]
            dest[:, base + g * HD : base + (g + 1) * HD] = (dk * SCALE).astype(bf16)
            dest[:, base + (2 + g) * HD : base + (3 + g) * HD] = dv.astype(bf16)
        if r == 0:
            for copy in copies:
                copy.start()
    for copy in copies:
        copy.wait()


def join_kernel(core, got, in_dq, in_dk, in_dv, full_dq, full_dk, full_dv, sems):
    half = 2 * HD
    other = 1 - core[0]
    copies = []
    for i, (full, start, width) in enumerate(
        ((full_dq, 0, 2 * QR), (full_dk, 2 * QR, half), (full_dv, 2 * QR + half, half))
    ):
        place = full.at[:, pl.ds(pl.multiple_of(other * width, width), width)]
        copies.append(pltpu.make_async_copy(got.at[:, start : start + width], place, sems.at[i]))
    for copy in copies:
        copy.start()
    for copy in copies:
        copy.wait()


def same_kernel(x, y, o, p):
    pass


def shard_kernel(core, k, v, o):
    rows = k.shape[0]
    cols = pl.ds(pl.multiple_of(core[0] * 2 * HD, 2 * HD), 2 * HD)
    shard = jnp.concatenate([k[:, cols], v[:, cols]], 1)
    for i in range(o.shape[0] // rows):
        o[i * rows : (i + 1) * rows, :] = shard


def sum_blocks_kernel(a, b, c, d, back_in, o, back):
    o[...] = (a[...] + b[...].astype(f32) + c[...].astype(f32) + d[...].astype(f32)).astype(bf16)


def sum_copies_kernel(x, o):
    rows = 16
    total = x[0:rows, :].astype(f32)
    for i in range(1, x.shape[0] // rows):
        total += x[i * rows : (i + 1) * rows, :].astype(f32)
    total = total.astype(bf16)
    for i in range(o.shape[0] // rows):
        o[i * rows : (i + 1) * rows, :] = total


def sum_samples_kernel(x, dk, dv):
    rows = 16
    half = 2 * HD
    for c in range(2):
        total = x[c * rows : (c + 1) * rows, :].astype(f32)
        for y in range(1, 4):
            at = (2 * y + c) * rows
            total += x[at : at + rows, :].astype(f32)
        dk[:, c * half : (c + 1) * half] = total[:, :half]
        dv[:, c * half : (c + 1) * half] = total[:, half:]


def simple(kernel, out_shape, name, *args, in_specs=None, out_specs=None, limit=16, **options):
    single = not isinstance(out_shape, tuple)
    return pl.pallas_call(
        kernel,
        out_shape=out_shape,
        in_specs=in_specs or [VMEM] * len(args),
        out_specs=out_specs or (VMEM if single else (VMEM,) * len(out_shape)),
        compiler_params=pltpu.CompilerParams(vmem_limit_bytes=int(limit * 2**20)),
        name=name,
        **options,
    )(*args)


def cost(rows):
    return pl.CostEstimate(
        flops=5 * 2 * rows * 4 * QR * HD, bytes_accessed=8 * 2**20, transcendentals=rows * 4 * QR
    )


PARAMS = pltpu.CompilerParams(vmem_limit_bytes=24 * 2**20)


def body(resp_q, resp_k, resp_v, resp_do, resp_out, resp_lse, prompt_k, prompt_v, resp_lengths):
    core = lax.axis_index("core").astype(jnp.int32)
    rows = prompt_k.shape[0]
    outer = ("yl", "zh", "zl")
    inner = "x"

    shards = simple(
        shard_kernel,
        jax.ShapeDtypeStruct((16 * rows, 4 * HD), bf16),
        "shards",
        core[None],
        prompt_k,
        prompt_v,
        in_specs=[SMEM, VMEM, VMEM],
        limit=61,
    )
    kv0 = lax.all_to_all(shards, outer, 0, 0, tiled=True)
    send, mine = prep(
        core,
        resp_lengths,
        resp_q[0],
        resp_do[0],
        resp_out[0],
        resp_k[0],
        resp_v[0],
        resp_lse[0].T,
        shards,
    )
    kv0, send = simple(
        same_kernel,
        (jax.ShapeDtypeStruct(kv0.shape, bf16), jax.ShapeDtypeStruct(send.shape, bf16)),
        "gathered_and_prepared",
        kv0,
        send,
        in_specs=[ANY, ANY],
        out_specs=(ANY, ANY),
        input_output_aliases={0: 0, 1: 1},
        limit=62.25,
    )
    recv = lax.ppermute(send, "core", [(0, 1), (1, 0)])

    def along(value, flip):
        return lax.ppermute(value, inner, [(i, i ^ flip) for i in range(4)])

    block_rows = 16 * rows
    blocks = [along(kv0, flip) for flip in FLIPS]
    dq_shape = jax.ShapeDtypeStruct((2, 2, QR, HD), f32)
    part_shape = jax.ShapeDtypeStruct((block_rows, 4 * HD), bf16)
    options = dict(compiler_params=PARAMS)
    dq, part1 = pl.pallas_call(
        first_kernel,
        out_shape=(dq_shape, part_shape),
        in_specs=[VMEM] * 3,
        out_specs=(VMEM,) * 2,
        cost_estimate=cost(block_rows),
        name="far_block",
        **options,
    )(mine, recv, blocks[0])
    part1 = along(part1, FLIPS[0])
    dq, part2, part3 = pl.pallas_call(
        middle_kernel,
        out_shape=(dq_shape, part_shape, part_shape),
        in_specs=[VMEM] * 5,
        out_specs=(VMEM,) * 3,
        input_output_aliases={4: 0},
        cost_estimate=cost(2 * block_rows),
        name="near_blocks",
        **options,
    )(mine, recv, blocks[1], blocks[2], dq)
    part2 = along(part2, FLIPS[1])
    part3 = along(part3, FLIPS[2])
    narrow = jax.ShapeDtypeStruct((R, KVH * HD), bf16)
    back, part0, full_dq, full_dk, full_dv = pl.pallas_call(
        last_kernel,
        out_shape=(
            jax.ShapeDtypeStruct((R, 2 * QR + 4 * HD), bf16),
            jax.ShapeDtypeStruct((block_rows, 4 * HD), f32),
            jax.ShapeDtypeStruct((R, H * HD), bf16),
            narrow,
            narrow,
        ),
        in_specs=[SMEM] + [VMEM] * 4 + [ANY],
        out_specs=(VMEM, VMEM, ANY, ANY, ANY),
        scratch_shapes=[
            pltpu.VMEM((2, 2, QR, HD), f32),
            pltpu.VMEM((R, 2 * QR), bf16),
            pltpu.VMEM((R, 4 * HD), bf16),
            pltpu.SemaphoreType.DMA((3,)),
        ],
        cost_estimate=cost(block_rows + R),
        name="own_block_and_own_keys",
        **options,
    )(core[None], mine, recv, kv0, dq, part1)
    total, back = simple(
        sum_blocks_kernel,
        (part_shape, jax.ShapeDtypeStruct(back.shape, bf16)),
        "sum_blocks",
        part0,
        part1,
        part3,
        part2,
        back,
        in_specs=[VMEM] * 4 + [ANY],
        out_specs=(VMEM, ANY),
        input_output_aliases={4: 1},
    )
    got = lax.ppermute(back, "core", [(0, 1), (1, 0)])
    total = lax.all_to_all(total, outer, 0, 0, tiled=True)
    total = simple(
        sum_copies_kernel, jax.ShapeDtypeStruct((8 * rows, 4 * HD), bf16), "sum_copies", total
    )
    total = lax.all_to_all(total, ("yh", "core"), 0, 0, tiled=True)
    final = jax.ShapeDtypeStruct((rows, KVH * HD), f32)
    prompt_dk, prompt_dv = simple(sum_samples_kernel, (final, final), "sum_samples", total)
    resp_dq, resp_dk, resp_dv = simple(
        join_kernel,
        (jax.ShapeDtypeStruct((R, H * HD), bf16), narrow, narrow),
        "join",
        core[None],
        got,
        full_dq,
        full_dk,
        full_dv,
        in_specs=[SMEM] + [ANY] * 4,
        out_specs=(ANY,) * 3,
        scratch_shapes=[pltpu.SemaphoreType.DMA((3,))],
        input_output_aliases={2: 0, 3: 1, 4: 2},
    )
    return resp_dq[None], resp_dk[None], resp_dv[None], prompt_dk, prompt_dv


def solution(mesh):
    fine = Mesh(mesh.devices.reshape(4, 2, 4, 2, 4, 2), AXES)
    both = P(AXES, None, None)
    prefix = P(("x", "yl", "zh", "zl"), None)
    return jax.shard_map(
        body,
        mesh=fine,
        in_specs=(both,) * 6 + (prefix, prefix, P(AXES)),
        out_specs=(both, both, both, prefix, prefix),
        check_vma=False,
    )
```
